512 devices in a mesh: gx: 32 (over y, x), gy: 16 (over z, core).
Axes of the slice: x: 4, y: 8, z: 8, core: 2. Of those that a mesh axis runs over, the one named last changes fastest.
Arguments:
- residual_in: float32 [448, 224, 336], P('gx', 'gy'), may hold values from -8 to 8
Outputs:
- correction: float32 [448, 224, 336], P('gx', 'gy')
- coarse_correction: float32 [64, 32, 48], P('gx', 'gy')
The draws below stay inside these ranges and needn't reach their ends.
All inputs are finite; a program needn't handle non-finite values.
Results may differ from the reference program's by a relative error of at most 0.0003.
Values sent between devices are 32-bit elements; how exact they have to be, the bound alone decides.
No kernel may reach another device: no remote copies, remote signals or barrier semaphores. Data moves between devices by JAX's collectives and lax.ppermute only.
A program may use at most 64 MiB of HBM per device.

```python
import math
import jax
import jax.numpy as jnp
import numpy as np
from jax import lax

SWEEPS = 2
NX = 448
NY = 224
NZ = 336


def draw_residual_in(key, part):
    key = jax.random.fold_in(key, 5)
    return jax.random.truncated_normal(key, -6.0, 6.0, (NX, NY, NZ), jnp.float32)


def setup_inputs(seed: int = 0) -> dict:
    streams_of = jax.random.split(jax.random.key(seed), 2)
    return {
        "residual_in": draw_residual_in(jax.random.fold_in(streams_of[1], 71), 0),
    }


spectral_radius_bound = lax.Precision.HIGHEST
theta_cheb = 1.125
delta_cheb = 0.875
start_points = [-0.8717401485096066, -0.5917001814331423, -0.2092992179024789, 0.2092992179024789, 0.5917001814331423, 0.8717401485096066]

def legendre_pair(value):
    before, now = (1.0, value)
    for order in range(1, 7):
        before, now = (now, ((2 * order + 1) * value * now - order * before) / (order + 1))
    return (now, before)

def lobatto_tables():
    point_list = [-1.0]
    for guess in start_points:
        place = guess
        for newton in range(4):
            seventh, sixth = legendre_pair(place)
            slope = 7.0 * (place * seventh - sixth) / (place * place - 1.0)
            curve = (2.0 * place * slope - 56.0 * seventh) / (1.0 - place * place)
            place = place - slope / curve
        point_list.append(place)
    point_list.append(1.0)
    sample_nodes_list = np.array(point_list)
    values = np.array([legendre_pair(place)[0] for place in point_list])
    weights = 2.0 / (56.0 * values * values)
    derivative = np.zeros((8, 8))
    for i in range(8):
        for j in range(8):
            if i != j:
                derivative[i, j] = values[i] / (values[j] * (sample_nodes_list[i] - sample_nodes_list[j]))
    derivative[0, 0] = -14.0
    derivative[7, 7] = 14.0
    stiffness = derivative.T @ (weights[:, None] * derivative)
    return (sample_nodes_list, weights, stiffness)

def assemble(elements, stiffness, weights):
    width = 7 * elements + 1
    assembled = np.zeros((width, width))
    masses = np.zeros(width)
    for e in range(elements):
        assembled[7 * e:7 * e + 8, 7 * e:7 * e + 8] += stiffness
        masses[7 * e:7 * e + 8] += weights
    return (assembled, masses)

def mass_vector(elements, weights):
    masses = np.tile(weights[:7], elements)
    masses[7::7] += weights[7]
    return masses

def jacobi_eigen(matrix):
    order = matrix.shape[0]
    work = [[float(matrix[i, j]) for j in range(order)] for i in range(order)]
    vectors = [[1.0 if i == j else 0.0 for j in range(order)] for i in range(order)]
    for sweep in range(12):
        for p in range(order):
            for q in range(p + 1, order):
                angle = 0.5 * math.atan2(2.0 * work[p][q], work[q][q] - work[p][p])
                cosine = math.cos(angle)
                sine = math.sin(angle)
                for k in range(order):
                    left, right = (work[k][p], work[k][q])
                    work[k][p] = cosine * left - sine * right
                    work[k][q] = sine * left + cosine * right
                for k in range(order):
                    left, right = (work[p][k], work[q][k])
                    work[p][k] = cosine * left - sine * right
                    work[q][k] = sine * left + cosine * right
                for k in range(order):
                    left, right = (vectors[k][p], vectors[k][q])
                    vectors[k][p] = cosine * left - sine * right
                    vectors[k][q] = sine * left + cosine * right
    return (np.array([work[i][i] for i in range(order)]), np.array(vectors))

def schwarz_basis():
    sample_nodes_list, weights, stiffness = lobatto_tables()
    assembled, masses = assemble(3, stiffness, weights)
    block_stiff = assembled[6:16, 6:16]
    inv_root = 1.0 / np.sqrt(masses[6:16])
    eigen_vals, eigen_vecs = jacobi_eigen(inv_root[:, None] * block_stiff * inv_root[None, :])
    return (inv_root[:, None] * eigen_vecs, eigen_vals)

def sine_table(vertex, modes_in, elements):
    operator_output = vertex[:, None] * modes_in[None, :] % (2 * elements)
    angles = jnp.pi * modes_in.astype(jnp.float32) / elements
    entries = jnp.sqrt(2.0 / elements) * jnp.sin(jnp.pi * operator_output.astype(jnp.float32) / elements)
    entries = entries / jnp.sqrt((4.0 + 2.0 * jnp.cos(angles)) / 3.0)[None, :]
    return jnp.where(modes_in[None, :] > 0, entries, 0.0)

def coarse_eigen(modes_in, elements):
    angles = jnp.pi * modes_in.astype(jnp.float32) / elements
    return jnp.where(modes_in > 0, 3.0 * (1.0 - jnp.cos(angles)) / (4.0 + 2.0 * jnp.cos(angles)), 1.0)

def stiff_along(nodal, axis, stiffness):
    moved = jnp.moveaxis(nodal, axis, 0)
    elements = moved.shape[0] // 7
    trailing = moved.shape[1:]
    blocks = moved.reshape((elements, 7) + trailing)
    next_nodes = jnp.concatenate([moved[7::7], jnp.zeros((1,) + trailing, moved.dtype)], axis=0)
    stacked = jnp.concatenate([blocks, next_nodes[:, None]], axis=1)
    operator_output = jnp.einsum('ij,ej...->ei...', stiffness, stacked, precision=spectral_radius_bound)
    result = operator_output[:, :7]
    result = result.at[1:, 0].add(operator_output[:-1, 7])
    return jnp.moveaxis(result.reshape(moved.shape), 0, axis)

def operate(nodal, interior, stiffness, mass_x, mass_y, mass_z):
    summed = stiff_along(nodal, 0, stiffness) * mass_y[None, :, None] * mass_z[None, None, :]
    summed = summed + mass_x[:, None, None] * stiff_along(nodal, 1, stiffness) * mass_z[None, None, :]
    summed = summed + (mass_x[:, None] * mass_y[None, :])[:, :, None] * stiff_along(nodal, 2, stiffness)
    return interior * summed

def schwarz(nodal, interior, eigen_basis, eigen_vals):
    nodes_x, nodes_y, nodes_z = nodal.shape
    cells_horizontal, elems_y, element_tally_along_height = (nodes_x // 7, nodes_y // 7, nodes_z // 7)
    padded = jnp.pad(nodal, ((1, 2), (1, 2), (1, 2)))
    take_y = np.arange(elems_y)[:, None] * 7 + np.arange(10)[None, :]
    take_z = np.arange(element_tally_along_height)[:, None] * 7 + np.arange(10)[None, :]
    denominator = eigen_vals[:, None, None, None, None] + eigen_vals[None, None, :, None, None] + eigen_vals[None, None, None, None, :]
    kept_rows = eigen_basis[1:8]

    def one_slab(slab):
        block = lax.dynamic_slice_in_dim(padded, 7 * slab, 10, 0)
        block = block[:, take_y][:, :, :, take_z]
        coeffs = jnp.einsum('ma,mpnqo->apnqo', eigen_basis, block, precision=spectral_radius_bound)
        coeffs = jnp.einsum('nb,apnqo->apbqo', eigen_basis, coeffs, precision=spectral_radius_bound)
        coeffs = jnp.einsum('oc,apbqo->apbqc', eigen_basis, coeffs, precision=spectral_radius_bound)
        coeffs = coeffs / denominator
        coeffs = jnp.einsum('ma,apbqc->mpbqc', kept_rows, coeffs, precision=spectral_radius_bound)
        coeffs = jnp.einsum('nb,mpbqc->mpnqc', kept_rows, coeffs, precision=spectral_radius_bound)
        coeffs = jnp.einsum('oc,mpnqc->mpnqo', kept_rows, coeffs, precision=spectral_radius_bound)
        return coeffs.reshape(7, nodes_y, nodes_z)
    slabs = lax.map(one_slab, jnp.arange(cells_horizontal, dtype=jnp.int32))
    return interior * slabs.reshape(nodes_x, nodes_y, nodes_z)

def restrict_along(nodal, axis, sample_nodes_list):
    moved = jnp.moveaxis(nodal, axis, 0)
    elements = moved.shape[0] // 7
    trailing = moved.shape[1:]
    blocks = moved.reshape((elements, 7) + trailing)
    weight_low = jnp.asarray((1.0 - sample_nodes_list[:7]) / 2.0, jnp.float32)
    weight_high = jnp.asarray((1.0 + sample_nodes_list[:7]) / 2.0, jnp.float32)
    from_low = jnp.einsum('m,em...->e...', weight_low, blocks, precision=spectral_radius_bound)
    from_high = jnp.einsum('m,em...->e...', weight_high, blocks, precision=spectral_radius_bound)
    empty_matrix_line = jnp.zeros((1,) + trailing, moved.dtype)
    result = jnp.concatenate([from_low, empty_matrix_line], axis=0) + jnp.concatenate([empty_matrix_line, from_high], axis=0)
    return jnp.moveaxis(result, 0, axis)

def prolong_along(coarse, axis, sample_nodes_list):
    moved = jnp.moveaxis(coarse, axis, 0)
    elements = moved.shape[0] - 1
    trailing = moved.shape[1:]
    shape_w = (1, 7) + (1,) * len(trailing)
    weight_low = jnp.asarray((1.0 - sample_nodes_list[:7]) / 2.0, jnp.float32).reshape(shape_w)
    weight_high = jnp.asarray((1.0 + sample_nodes_list[:7]) / 2.0, jnp.float32).reshape(shape_w)
    result = weight_low * moved[:-1][:, None] + weight_high * moved[1:][:, None]
    return jnp.moveaxis(result.reshape((7 * elements,) + trailing), 0, axis)

def reference(residual_in):
    sample_nodes_list, weights, stiffness_np = lobatto_tables()
    basis_np, vals_np = schwarz_basis()
    stiffness = jnp.asarray(stiffness_np, jnp.float32)
    eigen_basis = jnp.asarray(basis_np, jnp.float32)
    eigen_vals = jnp.asarray(vals_np, jnp.float32)
    nodes_x, nodes_y, nodes_z = residual_in.shape
    cells_horizontal, elems_y, element_tally_along_height = (nodes_x // 7, nodes_y // 7, nodes_z // 7)
    mass_x = jnp.asarray(mass_vector(cells_horizontal, weights), jnp.float32)
    mass_y = jnp.asarray(mass_vector(elems_y, weights), jnp.float32)
    mass_z = jnp.asarray(mass_vector(element_tally_along_height, weights), jnp.float32)
    interior = ((jnp.arange(nodes_x) > 0)[:, None, None] & (jnp.arange(nodes_y) > 0)[None, :, None] & (jnp.arange(nodes_z) > 0)[None, None, :]).astype(jnp.float32)
    source = interior * residual_in
    sigma_ratio = theta_cheb / delta_cheb
    rho_now = 1.0 / sigma_ratio
    direction = schwarz(source, interior, eigen_basis, eigen_vals) / theta_cheb
    approx = direction
    remain = source - operate(direction, interior, stiffness, mass_x, mass_y, mass_z)
    for step in range(1, SWEEPS):
        rho_next = 1.0 / (2.0 * sigma_ratio - rho_now)
        direction = rho_next * rho_now * direction + 2.0 * rho_next / delta_cheb * schwarz(remain, interior, eigen_basis, eigen_vals)
        approx = approx + direction
        remain = remain - operate(direction, interior, stiffness, mass_x, mass_y, mass_z)
        rho_now = rho_next
    coarse_residual_vector = restrict_along(restrict_along(restrict_along(remain, 0, sample_nodes_list), 1, sample_nodes_list), 2, sample_nodes_list)
    coarse_residual_vector = coarse_residual_vector[:, :, :element_tally_along_height]
    first_axis_table = sine_table(jnp.arange(cells_horizontal + 1), jnp.arange(cells_horizontal), cells_horizontal)
    table_y = sine_table(jnp.arange(elems_y + 1), jnp.arange(elems_y), elems_y)
    table_z = sine_table(jnp.arange(element_tally_along_height), jnp.arange(element_tally_along_height), element_tally_along_height)
    mode_eigenvalues = jnp.einsum('wst,wo->ost', coarse_residual_vector, first_axis_table, precision=spectral_radius_bound)
    mode_eigenvalues = jnp.einsum('aqm,qb->abm', mode_eigenvalues, table_y, precision=spectral_radius_bound)
    mode_eigenvalues = jnp.einsum('abm,mk->abk', mode_eigenvalues, table_z, precision=spectral_radius_bound)
    denominator = coarse_eigen(jnp.arange(cells_horizontal), cells_horizontal)[:, None, None] + coarse_eigen(jnp.arange(elems_y), elems_y)[None, :, None] + coarse_eigen(jnp.arange(element_tally_along_height), element_tally_along_height)[None, None, :]
    scaled = mode_eigenvalues / denominator
    coarse_solution_vector = jnp.einsum('abk,mk->abm', scaled, table_z, precision=spectral_radius_bound)
    coarse_solution_vector = jnp.einsum('abm,qb->aqm', coarse_solution_vector, table_y, precision=spectral_radius_bound)
    coarse_solution_vector = jnp.einsum('bek,wb->wek', coarse_solution_vector, first_axis_table, precision=spectral_radius_bound)
    padded_sol = jnp.concatenate([coarse_solution_vector, jnp.zeros((cells_horizontal + 1, elems_y + 1, 1), jnp.float32)], axis=2)
    fine_level_portion = prolong_along(prolong_along(prolong_along(padded_sol, 2, sample_nodes_list), 1, sample_nodes_list), 0, sample_nodes_list)
    correction = approx + interior * fine_level_portion
    return (correction, coarse_solution_vector[:cells_horizontal, :elems_y, :])
```

```python
import math

import jax
import jax.numpy as jnp
import ml_dtypes
import numpy as np
from jax import lax
from jax.experimental import pallas as pl
from jax.experimental.pallas import tpu as pltpu
from jax.sharding import PartitionSpec as P

theta_cheb = 1.125
delta_cheb = 0.875
start_points = [
    -0.8717401485096066,
    -0.5917001814331423,
    -0.2092992179024789,
    0.2092992179024789,
    0.5917001814331423,
    0.8717401485096066,
]


def legendre_pair(value):
    before, now = (1.0, value)
    for order in range(1, 7):
        before, now = (now, ((2 * order + 1) * value * now - order * before) / (order + 1))
    return (now, before)


def lobatto_tables():
    point_list = [-1.0]
    for guess in start_points:
        place = guess
        for newton in range(4):
            seventh, sixth = legendre_pair(place)
            slope = 7.0 * (place * seventh - sixth) / (place * place - 1.0)
            curve = (2.0 * place * slope - 56.0 * seventh) / (1.0 - place * place)
            place = place - slope / curve
        point_list.append(place)
    point_list.append(1.0)
    sample_nodes_list = np.array(point_list)
    values = np.array([legendre_pair(place)[0] for place in point_list])
    weights = 2.0 / (56.0 * values * values)
    derivative = np.zeros((8, 8))
    for i in range(8):
        for j in range(8):
            if i != j:
                derivative[i, j] = values[i] / (
                    values[j] * (sample_nodes_list[i] - sample_nodes_list[j])
                )
    derivative[0, 0] = -14.0
    derivative[7, 7] = 14.0
    stiffness = derivative.T @ (weights[:, None] * derivative)
    return (sample_nodes_list, weights, stiffness)


def assemble(elements, stiffness, weights):
    width = 7 * elements + 1
    assembled = np.zeros((width, width))
    masses = np.zeros(width)
    for e in range(elements):
        assembled[7 * e : 7 * e + 8, 7 * e : 7 * e + 8] += stiffness
        masses[7 * e : 7 * e + 8] += weights
    return (assembled, masses)


def jacobi_eigen(matrix):
    order = matrix.shape[0]
    work = [[float(matrix[i, j]) for j in range(order)] for i in range(order)]
    vectors = [[1.0 if i == j else 0.0 for j in range(order)] for i in range(order)]
    for sweep in range(12):
        for p in range(order):
            for q in range(p + 1, order):
                angle = 0.5 * math.atan2(2.0 * work[p][q], work[q][q] - work[p][p])
                cosine = math.cos(angle)
                sine = math.sin(angle)
                for k in range(order):
                    left, right = (work[k][p], work[k][q])
                    work[k][p] = cosine * left - sine * right
                    work[k][q] = sine * left + cosine * right
                for k in range(order):
                    left, right = (work[p][k], work[q][k])
                    work[p][k] = cosine * left - sine * right
                    work[q][k] = sine * left + cosine * right
                for k in range(order):
                    left, right = (vectors[k][p], vectors[k][q])
                    vectors[k][p] = cosine * left - sine * right
                    vectors[k][q] = sine * left + cosine * right
    return (np.array([work[i][i] for i in range(order)]), np.array(vectors))


def schwarz_basis():
    sample_nodes_list, weights, stiffness = lobatto_tables()
    assembled, masses = assemble(3, stiffness, weights)
    block_stiff = assembled[6:16, 6:16]
    inv_root = 1.0 / np.sqrt(masses[6:16])
    eigen_vals, eigen_vecs = jacobi_eigen(inv_root[:, None] * block_stiff * inv_root[None, :])
    return (inv_root[:, None] * eigen_vecs, eigen_vals)


def forward_table(elements, eigen_basis):
    matrix = np.zeros((10 * elements, 7 * elements + 4))
    for j in range(elements):
        matrix[10 * j : 10 * j + 10, 7 * j + 1 : 7 * j + 11] = eigen_basis.T
    return matrix


def backward_table(elements, eigen_basis):
    matrix = np.zeros((7 * elements, 10 * elements))
    for j in range(elements):
        matrix[7 * j : 7 * j + 7, 10 * j : 10 * j + 10] = eigen_basis[1:8]
    return matrix


def injection_coefficients(elements, sample_nodes_list):
    matrix = np.zeros((elements + 1, 7 * elements))
    for e in range(elements):
        for m in range(7):
            matrix[e, 7 * e + m] += (1.0 - sample_nodes_list[m]) / 2.0
            matrix[e + 1, 7 * e + m] += (1.0 + sample_nodes_list[m]) / 2.0
    return matrix


def sine_modes(vertex, elements):
    modes = np.arange(elements)
    angles = np.pi * modes / elements
    entries = np.sqrt(2.0 / elements) * np.sin(
        np.pi * (np.asarray(vertex)[:, None] * modes[None, :] % (2 * elements)) / elements
    )
    entries = entries / np.sqrt((4.0 + 2.0 * np.cos(angles)) / 3.0)[None, :]
    return np.where(modes[None, :] > 0, entries, 0.0)


def coarse_eigen(elements):
    angles = np.pi * np.arange(elements) / elements
    return np.where(
        np.arange(elements) > 0, 3.0 * (1.0 - np.cos(angles)) / (4.0 + 2.0 * np.cos(angles)), 1.0
    )


class Pack:
    def __init__(self, width):
        self.width, self.rows, self.blocks = (width, 0, [])

    def put(self, row, lane, matrix):
        self.blocks.append((row, lane, np.asarray(matrix)))
        self.rows = max(self.rows, row + -(-matrix.shape[0] // 16) * 16)
        return (slice(row, row + matrix.shape[0]), slice(lane, lane + matrix.shape[1]))

    def add(self, matrix, count=2):
        parts = []
        for _ in range(count):
            parts.append(np.asarray(matrix).astype(ml_dtypes.bfloat16))
            matrix = matrix - parts[-1].astype(np.float64)
        row, step = (self.rows, max(128, -(-matrix.shape[1] // 128) * 128))
        places = []
        for number, part in enumerate(parts):
            if step * count <= self.width:
                places.append(self.put(row, step * number, part))
            else:
                places.append(self.put(self.rows, 0, part))
        return tuple(places)

    def array(self, dtype, rows=0):
        whole = np.zeros((max(self.rows, rows), self.width), dtype)
        for row, lane, matrix in self.blocks:
            whole[row : row + matrix.shape[0], lane : lane + matrix.shape[1]] = matrix
        return whole


def parts(ref, places):
    return tuple(ref[place] for place in places)


def whole(ref, places, rows=None):
    if rows is not None:
        places = [(rows, lanes) for _, lanes in places]
    high, middle, low = (ref[place].astype(jnp.float32) for place in places)
    return high + (middle + low)


def split(value):
    high = value.astype(jnp.bfloat16)
    return (high, (value - high.astype(jnp.float32)).astype(jnp.bfloat16))


def dot3(left, right):
    def mul(a, b):
        return jnp.dot(a, b, preferred_element_type=jnp.float32)

    return mul(left[0], right[0]) + (mul(left[0], right[1]) + mul(left[1], right[0]))


def dot32(left, right):
    return jnp.dot(
        left, right, precision=lax.Precision.HIGHEST, preferred_element_type=jnp.float32
    )


NONE = None
OWN = list(range(14)) + [NONE, NONE]
X_RING = OWN[:14] + [14, 15, -1]
Y_RING = OWN + [14, 15, -1] + [NONE] * 5
EDGE = [0, 1, NONE, 13] + [NONE] * 4
VERTICES = [(0, 0), (0, 1), (1, 0), (1, 1), (0, 2), (1, 2), (2, 0), (2, 1), (2, 2)]
LOADER_ROOM = 48
EARLY_ROWS = 20 * 1024


def pick(matrix, rows, columns, row_zero, column_zero):
    result = np.zeros((len(rows), len(columns)))
    for i, row in enumerate(rows):
        for j, column in enumerate(columns):
            if row is not None and column is not None:
                result[i, j] = matrix[row + row_zero, column + column_zero]
    return result


def pick_vector(vector, slots, zero):
    return np.array([0.0 if slot is None else vector[slot + zero] for slot in slots])


class Tables:
    def __init__(self, elements_z, count_x, count_y):
        points, weights, stiffness = lobatto_tables()
        basis, values = schwarz_basis()
        nodes_z = 7 * elements_z
        half = elements_z // 2
        self.cut = cut = (7 * half) // 128 * 128
        self.first = first = min(256, nodes_z)
        self.stiffness = stiffness
        smoother, second = (Pack(512), Pack(512))
        mask_z = np.arange(nodes_z) > 0

        ahead = forward_table(2, basis)
        back = backward_table(2, basis)
        back_y = np.zeros((16, 20))
        back_y[:14] = back
        ahead_x = pick(ahead, range(20), X_RING, 0, 2)
        self.ahead_own = smoother.add(np.kron(ahead_x, pick(ahead, range(20), OWN, 0, 2)))
        ahead_edge = pick(ahead, range(20), Y_RING[16:], 0, 2)
        ahead_edge[:, 3] = -ahead[:, 2]
        ahead_edge[:, 4] = -(ahead[:, 9:16] @ stiffness[:7, 7])
        self.ahead_edge = smoother.add(np.kron(ahead_x, ahead_edge))
        self.back_xy = smoother.add(np.kron(back, back_y))
        all_ahead = forward_table(elements_z, basis)[:, 2 : 2 + nodes_z].T * mask_z[:, None]
        all_back = backward_table(elements_z, basis).T * mask_z[None, :]
        self.ahead_z, self.back_z, self.value_columns = ([], [], [])
        for low, high, base, stop in ((0, half, 0, first), (half, elements_z, cut, nodes_z)):
            modes, width = (slice(10 * low, 10 * high), 10 * (high - low))
            assert not all_ahead[:base, modes].any() and not all_ahead[stop:, modes].any()
            assert not all_back[modes, :base].any() and not all_back[modes, stop:].any()
            ahead_z, back_z = (np.zeros((stop - base, 256)), np.zeros((256, stop - base)))
            ahead_z[:, :width] = all_ahead[base:stop, modes]
            back_z[:width] = all_back[modes, base:stop]
            columns = np.ones((1, 256))
            columns[0, :width] = np.tile(values, high - low)
            self.ahead_z.append(smoother.add(ahead_z))
            self.back_z.append(smoother.add(back_z))
            self.value_columns.append(smoother.add(columns, 3))
        rows = np.add.outer(np.tile(values, 2), np.tile(values, 2)).reshape(400, 1)
        self.value_rows = smoother.add(rows, 3)

        pair, _ = assemble(2, stiffness, weights)
        _, mass = assemble(4, stiffness, weights)
        stiff_x = np.zeros((17, 21))
        stiff_x[:15, :15] = pair
        stiff_x[0, 0] += stiffness[7, 7]
        stiff_x[16, 0] = stiffness[6, 7]
        for row, column in ((0, 17), (16, 18), (14, 19), (15, 20)):
            stiff_x[row, column] = 1.0
        stiff_y = np.zeros((16, 16))
        stiff_y[:14, :14] = pair[:14, :14]
        stiff_y[0, 0] += stiffness[7, 7]
        edge_y = np.zeros((8, 16))
        edge_y[0, 0:8], edge_y[1, 0:8], edge_y[2, 0] = (stiffness[0], stiffness[1], 1.0)
        edge_y[3, 7:14], edge_y[4, 7:14] = (stiffness[6, :7], stiffness[7, :7])
        mass_x, mass_y = (pick_vector(mass, X_RING, 7), pick_vector(mass, OWN, 7))
        mass_edge = pick_vector(mass, EDGE, 7)
        batches = ((0, 8), (8, 16), (16, 17))
        self.batches = batches
        self.edge_x = second.add(np.kron(stiff_x, np.diag(mass_edge)))
        self.edge_y = [
            second.add(np.kron(np.diag(mass_x[low:high]), edge_y)) for low, high in batches
        ]
        self.own_x = [
            second.add(np.kron(stiff_x, np.diag(mass_y[low : low + 8]))) for low in (0, 8)
        ]
        self.own_y = [
            second.add(np.kron(np.diag(mass_x[low:high]), stiff_y)) for low, high in batches
        ]
        self.mass_edge = second.add(np.outer(mass_x, mass_edge).reshape(-1, 1), 3)
        self.mass_own = second.add(np.outer(mass_x, mass_y).reshape(-1, 1), 3)
        stiff_z, line_z = assemble(elements_z, stiffness, weights)
        stiff_z, line_z = (stiff_z[:nodes_z, :nodes_z], line_z[:nodes_z])
        self.mass_z = second.add(line_z[None, :], 3)
        low_z, high_z = (stiff_z[:first, :first].copy(), stiff_z[cut:, cut:].copy())
        low_z[:, 7 * half :] = 0.0
        high_z[:, : 7 * half - cut] = 0.0
        self.stiff_z = [second.add(low_z), second.add(high_z)]

        stiff3, mass3 = assemble(3, stiffness, weights)
        inject = np.zeros((4, 22))
        inject[:, :21] = injection_coefficients(3, points)
        inject[3, 21] = 1.0

        def padded(matrix):
            wide = np.zeros((matrix.shape[0], 16))
            wide[:, :14] = matrix
            return wide

        drop = inject[:, 7:21]
        drop_mass = (inject * mass3[None, :])[:, 7:21]
        drop_stiff = (inject @ stiff3)[:, 7:21]
        self.drop_b = second.add(np.kron(drop, padded(drop)))
        across = np.kron(drop_stiff, padded(drop_mass)) + np.kron(drop_mass, padded(drop_stiff))
        self.drop_x = second.add(
            -np.concatenate([across, np.kron(drop_mass, padded(drop_mass))])
        )
        drop_z = injection_coefficients(elements_z, points)[:elements_z]
        phi_z = sine_modes(np.arange(elements_z), elements_z)
        masked_z = (drop_z * mask_z[None, :]).T
        modes_z = np.zeros((nodes_z, 384))
        for part, matrix in enumerate((masked_z, line_z[:, None] * masked_z, stiff_z @ masked_z)):
            for base in (128 * part, 128 * part + 64):
                modes_z[:, base : base + elements_z] = matrix @ phi_z
        self.modes_z = second.add(modes_z)

        sides_x, sides_y = (count_x // 2, count_y // 2)
        phi_x = sine_modes(np.arange(count_x + 1), count_x)
        phi_y = sine_modes(np.arange(count_y + 1), count_y)
        lam_x, lam_y = (coarse_eigen(count_x), coarse_eigen(count_y))
        assert elements_z <= 64
        eigen_z = coarse_eigen(elements_z)
        eye_x = np.eye(4)
        to_y = np.zeros((sides_y, sides_y, 4, 2, 4, 4))
        from_y = np.zeros((sides_y, 2, 16, sides_y, 4))
        eigen_yz = np.ones((sides_y, 2, 64))
        for place in range(sides_y):
            eigen_yz[place, :, :elements_z] = (
                lam_y[2 * place : 2 * place + 2, None] + eigen_z[None, :]
            )
            for j in range(4):
                if 2 * place + j - 1 >= 0:
                    row = phi_y[2 * place + j - 1].reshape(sides_y, 2)
                    to_y[place, :, :, :, :, j] = (
                        eye_x[None, :, None, :] * row[:, None, :, None]
                    )
            for number, (i, j) in enumerate(VERTICES):
                row = phi_y[2 * place + j].reshape(sides_y, 2)
                from_y[place, :, number, :, i] = row.T
        to_x = np.zeros((count_x, sides_x, 4))
        from_x = np.zeros((sides_x, 16, count_x))
        for place in range(sides_x):
            for i in range(4):
                if 2 * place + i - 1 >= 0:
                    to_x[:, place, i] = phi_x[2 * place + i - 1]
            from_x[place, :3] = phi_x[2 * place : 2 * place + 3]
        self.sent = sent = 4 * sides_y
        self.count_x = count_x
        height = -(-sent // 16) * 16
        places = Pack(512)
        for place in range(sides_y):
            rows = np.zeros((height + 48, 128))
            rows[:sent, :32] = to_y[place].reshape(sent, 32)
            rows[height : height + 32, :sent] = from_y[place].reshape(32, sent)
            rows[height + 32] = eigen_yz[place].ravel()
            places.add(rows, 3)
        self.height = height
        self.place_x_base = places.rows
        for place in range(sides_x):
            rows = np.zeros((16, 128))
            rows[:, :count_x] = from_x[place]
            places.add(rows, 3)
        lift = injection_coefficients(2, points)
        lift_xy = np.zeros((14, 16, 16))
        for number, (i, j) in enumerate(VERTICES):
            lift_xy[:, :14, number] = np.outer(lift[i], lift[j])
        lift_z, back_phi = (np.zeros((128, nodes_z)), np.zeros((128, elements_z)))
        for base in (0, 64):
            lift_z[base : base + elements_z] = phi_z.T @ drop_z * mask_z[None, :]
            back_phi[base : base + elements_z] = phi_z.T
        late = Pack(512)
        self.to_modes_x = late.put(0, 0, to_x.reshape(count_x, 4 * sides_x))
        self.lift_xy = late.put(0, 256, lift_xy.reshape(224, 16))
        self.eigen_x = late.put(0, 384, lam_x[:, None])
        self.lift_z = late.put(224, 0, lift_z)
        self.phi_z = late.put(224, 384, back_phi)

        self.late = late.array(np.float32)
        self.smoother_rows, self.second_rows = (smoother.rows, second.rows)
        self.places_base = smoother.rows + second.rows
        self.early = np.zeros((EARLY_ROWS, 512), ml_dtypes.bfloat16)
        stacked = [pack.array(ml_dtypes.bfloat16) for pack in (smoother, second, places)]
        used = np.concatenate(stacked)
        self.early[: used.shape[0]] = used
        self.place_parts = tuple(
            (slice(None), slice(128 * part, 128 * part + 128)) for part in range(3)
        )


def sides_of(places, sides):
    flags = []
    for axis in range(2):
        flags.append(jnp.where(places[axis] > 0, 1.0, 0.0))
        flags.append(jnp.where(places[axis] < sides[axis] - 1, 1.0, 0.0))
    return flags


def line_mask(flags):
    x = lax.broadcasted_iota(jnp.int32, (17, 16, 1), 0)
    y = lax.broadcasted_iota(jnp.int32, (17, 16, 1), 1)
    keep_x = jnp.where((x == 0) | (x == 16), flags[0], jnp.where(x >= 14, flags[1], 1.0))
    return keep_x * jnp.where(y == 0, flags[2], 1.0)


def edge_mask(flags):
    x = lax.broadcasted_iota(jnp.int32, (17, 8, 1), 0)
    slot = lax.broadcasted_iota(jnp.int32, (17, 8, 1), 1)
    keep_x = jnp.where((x == 0) | (x == 16), flags[0], jnp.where(x >= 14, flags[1], 1.0))
    return keep_x * jnp.where((slot == 2) | (slot == 3), flags[2], flags[3])


def own_mask(flags):
    x = lax.broadcasted_iota(jnp.int32, (14, 16, 1), 0)
    y = lax.broadcasted_iota(jnp.int32, (14, 16, 1), 1)
    return jnp.where(x == 0, flags[0], 1.0) * jnp.where(y == 0, flags[2], 1.0)


def join_z(low, high, cut):
    middle = low.shape[1]
    return jnp.concatenate(
        [low[:, :cut], low[:, cut:] + high[:, : middle - cut], high[:, middle - cut :]], axis=1
    )


def schwarz(modes, edge, tables, smoother):
    cut = tables.cut
    edge = split(edge.reshape(136, edge.shape[2]))
    modes = modes + dot3(parts(smoother, tables.ahead_edge), edge)
    rows = whole(smoother, tables.value_rows)
    halves = []
    for number, block in enumerate((modes[:, : tables.first], modes[:, cut:])):
        block = dot3(split(block), parts(smoother, tables.ahead_z[number]))
        block = block / (rows + whole(smoother, tables.value_columns[number]))
        halves.append(dot3(split(block), parts(smoother, tables.back_z[number])))
    return dot3(parts(smoother, tables.back_xy), split(join_z(*halves, cut)))


class Shape(tuple):
    dtype = jnp.float32


class HalfShape(Shape):
    dtype = jnp.bfloat16


def kernel_call(body, inputs, outputs, scratch=(), spaces={}, flops=0, moved=0, room=4):
    def kernel(*refs):
        last = len(inputs) + len(outputs)
        body(refs[: len(inputs)], refs[len(inputs) : last], refs[last:])

    return pl.pallas_call(
        kernel,
        out_shape=[jax.ShapeDtypeStruct(shape, shape.dtype) for shape in outputs],
        in_specs=[
            pl.BlockSpec(memory_space=spaces.get(number, pltpu.VMEM))
            for number in range(len(inputs))
        ],
        out_specs=[pl.BlockSpec(memory_space=pltpu.VMEM) for _ in outputs],
        scratch_shapes=list(scratch),
        compiler_params=pltpu.CompilerParams(vmem_limit_bytes=room * 1024 * 1024),
        cost_estimate=pl.CostEstimate(flops=flops, bytes_accessed=moved, transcendentals=0),
    )(*inputs)


def run_copies(pairs, semaphores):
    copies = [
        pltpu.make_async_copy(source, target, semaphores.at[number])
        for number, (source, target) in enumerate(pairs)
    ]
    for copy in copies:
        copy.start()
    for copy in copies:
        copy.wait()


def load_smoother(tables):
    def body(ins, outs, scratch):
        run_copies([(ins[0].at[0 : tables.smoother_rows], outs[0])], scratch[0])

    return body


def load_second(tables):
    def body(ins, outs, scratch):
        early, places, _ = ins
        base = tables.smoother_rows
        size = tables.height + 48
        row_y = pl.multiple_of(tables.places_base + size * places[1], 16)
        row_x = pl.multiple_of(tables.places_base + tables.place_x_base + 16 * places[0], 16)
        run_copies(
            [
                (early.at[base : base + tables.second_rows], outs[0]),
                (early.at[pl.ds(row_y, size)], outs[1]),
                (early.at[pl.ds(row_x, 16)], outs[2]),
            ],
            scratch[0],
        )

    return body


def first_x_rows(ins, outs, scratch):
    outs[0][...] = ins[0][...]
    outs[1][...] = ins[0][0:2]
    outs[2][...] = ins[0][13:14]


def first_y_rows(ins, outs, scratch):
    own, x_low, x_high, _ = ins
    for out, rows in zip(outs, (slice(0, 2), slice(13, 14))):
        out[0:14] = own[:, rows]
        out[14:16] = x_high[:, rows]
        out[16:17] = x_low[:, rows]


def own_modes(tables, sides):
    def body(ins, outs, scratch):
        places, own, x_low, x_high, smoother = ins
        (line,) = scratch
        nodes_z = own.shape[2]
        line[:, 14:16] = jnp.zeros((17, 2, nodes_z), jnp.float32)
        line[0:14, 0:14] = own[...]
        line[14:16, 0:14] = x_high[...]
        line[16:17, 0:14] = x_low[...]
        masked = line[...] * line_mask(sides_of(places, sides))
        outs[0][...] = masked
        rows = split(masked.reshape(272, nodes_z))
        outs[1][...] = dot3(parts(smoother, tables.ahead_own), rows)

    return body


def first_sweep(tables, sides):
    def body(ins, outs, scratch):
        places, modes, y_low, y_high, smoother = ins
        flags = sides_of(places, sides)
        nodes_z = modes.shape[1]
        edge = outs[1]
        edge[:, 0:2] = y_high[...]
        edge[:, 2:3] = y_low[...]
        edge[:, 3:8] = jnp.zeros((17, 5, nodes_z), jnp.float32)
        edge[...] = edge[...] * edge_mask(flags)
        result = schwarz(modes[...], edge[...], tables, smoother)
        result = result.reshape(14, 16, nodes_z) * (own_mask(flags) * (1.0 / theta_cheb))
        result = result[:, :14]
        outs[0][...] = result
        stiffness = tables.stiffness
        outs[2][0:2] = result[0:2]
        outs[3][0:1] = result[13:14]
        for row in range(2):
            outs[2][2 + row] = sum(float(stiffness[row, j]) * result[j] for j in range(8))
            outs[3][1 + row] = sum(float(stiffness[7 - row, j]) * result[7 + j] for j in range(7))

    return body


def fill_lines(line, own, x_low, x_high):
    line[:, 14:16] = jnp.zeros((21, 2, own.shape[2]), jnp.float32)
    line[0:14, 0:14] = own[...]
    line[14:16, 0:14] = x_high[0:2]
    line[16:19, 0:14] = x_low[...]
    line[19:21, 0:14] = x_high[2:4]


def apply_z(rows, tables, second):
    return join_z(
        dot3(split(rows[:, : tables.first]), parts(second, tables.stiff_z[0])),
        dot3(split(rows[:, tables.cut :]), parts(second, tables.stiff_z[1])),
        tables.cut,
    )


def edge_rows(tables):
    def body(ins, outs, scratch):
        own, x_low, x_high, second = ins
        line, edge, total = scratch
        nodes_z = own.shape[2]
        fill_lines(line, own, x_low, x_high)
        edge[...] = jnp.zeros((21, 8, nodes_z), jnp.float32)
        edge[:, 0:2] = line[:, 0:2]
        edge[:, 3:4] = line[:, 13:14]
        part = dot3(parts(second, tables.edge_x), split(edge[...].reshape(168, nodes_z)))
        total[...] = part.reshape(17, 8, nodes_z)
        for places, (low, high) in zip(tables.edge_y, tables.batches):
            rows = line[low:high].reshape(16 * (high - low), nodes_z)
            part = dot3(parts(second, places), split(rows))
            total[low:high] += part.reshape(high - low, 8, nodes_z)
        along = apply_z(edge[0:17].reshape(136, nodes_z), tables, second)
        result = total[...].reshape(136, nodes_z) * whole(second, tables.mass_z)
        result = result + whole(second, tables.mass_edge) * along
        total[...] = result.reshape(17, 8, nodes_z)
        outs[0][...] = total[:, 0:3]
        outs[1][...] = total[:, 3:5]

    return body


def own_rows(tables, sides):
    def body(ins, outs, scratch):
        own, x_low, x_high, second, places, source, smoother = ins
        line, total = scratch
        modes, from_b = outs
        nodes_z = own.shape[2]
        fill_lines(line, own, x_low, x_high)
        for number, place in enumerate(tables.own_x):
            rows = line[:, 8 * number : 8 * number + 8].reshape(168, nodes_z)
            part = dot3(parts(second, place), split(rows))
            total[:, 8 * number : 8 * number + 8] = part.reshape(17, 8, nodes_z)
        for place, (low, high) in zip(tables.own_y, tables.batches):
            rows = line[low:high].reshape(16 * (high - low), nodes_z)
            part = dot3(parts(second, place), split(rows))
            total[low:high] += part.reshape(high - low, 16, nodes_z)
        along = apply_z(line[0:17].reshape(272, nodes_z), tables, second)
        applied = total[...].reshape(272, nodes_z) * whole(second, tables.mass_z)
        applied = applied + whole(second, tables.mass_own) * along
        remain = (source[...] - applied.reshape(17, 16, nodes_z)) * line_mask(sides_of(places, sides))
        modes[...] = dot3(parts(smoother, tables.ahead_own), split(remain.reshape(272, nodes_z)))
        rows = source[0:14].reshape(224, nodes_z)
        from_b[...] = dot3(parts(second, tables.drop_b), split(rows))

    return body


def second_sweep(tables, sides, scale_old, scale_new):
    def body(ins, outs, scratch):
        places, own, modes, to_low, to_high, y_low, y_high, source, from_b = ins[:9]
        smoother, second, place_y = ins[9:]
        edge, update = scratch
        flags = sides_of(places, sides)
        nodes_z = own.shape[2]
        stiffness = tables.stiffness
        above = y_high[:, 2:3]
        edge[:, 0:1] = source[:, 0:1] - (
            y_high[:, 0:1] + to_high[:, 1:2] + float(stiffness[7, 7]) * above
        )
        edge[:, 1:2] = source[:, 1:2] - y_high[:, 1:2]
        edge[:, 2:3] = source[:, 2:3] - (y_low[:, 0:1] + float(stiffness[6, 7]) * to_low[:, 2:3])
        edge[:, 3:4] = y_low[:, 1:2]
        edge[:, 4:5] = above
        edge[:, 5:8] = jnp.zeros((17, 3, nodes_z), jnp.float32)
        result = schwarz(modes[...], edge[...] * edge_mask(flags), tables, smoother)
        update[...] = result.reshape(14, 16, nodes_z) * (own_mask(flags) * scale_new)
        update[:, 0:14] += (1.0 + scale_old) * own[...]
        outs[0][...] = update[:, 0:14]
        from_x = dot3(parts(second, tables.drop_x), split(update[...].reshape(224, nodes_z)))
        both = jnp.concatenate([from_b[...], from_x], axis=0)
        modes = dot3(split(both), parts(second, tables.modes_z))
        modes = modes[0:16, 0:128] + modes[16:32, 128:256] + modes[32:48, 256:384]
        left = lax.broadcasted_iota(jnp.int32, (16, 128), 1) < 64
        modes = jnp.concatenate([jnp.where(left, modes, 0.0), jnp.where(left, 0.0, modes)], axis=0)
        to_modes_y = whole(place_y, tables.place_parts, slice(0, tables.sent))[:, 0:32]
        outs[1][...] = dot32(to_modes_y, modes).reshape(outs[1].shape)

    return body


def sum_modes_y(ins, outs, scratch):
    outs[0][...] = jnp.broadcast_to(jnp.sum(ins[0][...], axis=0, keepdims=True), outs[0].shape)


def solve_modes(tables):
    def body(ins, outs, scratch):
        arrived, late, place_x, place_y = ins
        modes = dot32(late[tables.to_modes_x], arrived[...].reshape(-1, 128))
        row = tables.height + 32
        eigen_yz = whole(place_y, tables.place_parts, slice(row, row + 16))[0:1]
        modes = modes / (late[tables.eigen_x] + eigen_yz)
        back = dot32(whole(place_x, tables.place_parts)[0:8, 0 : tables.count_x], modes)
        outs[0][...] = jnp.broadcast_to(back[None, 0:4], outs[0].shape)

    return body


def finish(tables, sides):
    def body(ins, outs, scratch):
        places, arrived, approx, late, place_y = ins
        nodes_z = approx.shape[2]
        rows = slice(tables.height, tables.height + 32)
        from_modes_y = whole(place_y, tables.place_parts, rows)[:, 0 : tables.sent]
        vertices = dot3(split(from_modes_y), split(arrived[...].reshape(-1, 128)))
        left = lax.broadcasted_iota(jnp.int32, (16, 128), 1) < 64
        vertices = split(jnp.where(left, vertices[0:16], vertices[16:32]))
        coarse = dot3(vertices, split(late[tables.phi_z]))
        outs[1][0] = coarse[0:2]
        outs[1][1] = coarse[2:4]
        lines = dot3(vertices, split(late[tables.lift_z]))
        fine = dot3(split(late[tables.lift_xy]), split(lines))
        fine = fine.reshape(14, 16, nodes_z) * own_mask(sides_of(places, sides))
        outs[0][...] = approx[...] + fine[:, :14]

    return body


def shift(block, axis, distance):
    count = lax.axis_size(axis)
    route = [((i - distance) % count, i) for i in range(count)]
    if axis == "gx":
        route = [(i, j) for i, j in route if j - i == distance]
    return lax.ppermute(block, axis, route)


def per_device(residual_in):
    nodes_x, nodes_y, nodes_z = residual_in.shape
    assert nodes_x == 14 and nodes_y == 14 and nodes_z % 14 == 0
    sides = (lax.axis_size("gx"), lax.axis_size("gy"))
    places = jnp.stack([lax.axis_index("gx"), lax.axis_index("gy")]).astype(jnp.int32)
    elements_z = nodes_z // 7
    tables = Tables(elements_z, 2 * sides[0], 2 * sides[1])
    early, late = (jnp.asarray(tables.early), jnp.asarray(tables.late))
    sigma_ratio = theta_cheb / delta_cheb
    rho_now = 1.0 / sigma_ratio
    rho_next = 1.0 / (2.0 * sigma_ratio - rho_now)
    scalars = {0: pltpu.SMEM}

    def block(*shape):
        return Shape(shape + (nodes_z,))

    def scratch(*shape):
        return pltpu.VMEM(shape + (nodes_z,), jnp.float32)

    own, to_low, to_high = kernel_call(
        first_x_rows, [residual_in], [block(14, 14), block(2, 14), block(1, 14)]
    )
    x_low, x_high = (shift(to_high, "gx", 1), shift(to_low, "gx", -1))
    (smoother,) = kernel_call(
        load_smoother(tables),
        [early],
        [HalfShape((tables.smoother_rows, 512))],
        [pltpu.SemaphoreType.DMA((1,))],
        {0: pl.ANY},
        moved=6_000_000,
        room=LOADER_ROOM,
    )
    to_low, to_high = kernel_call(
        first_y_rows, [own, x_low, x_high, smoother], [block(17, 2), block(17, 1)]
    )
    y_low, y_high = (shift(to_high, "gy", 1), shift(to_low, "gy", -1))
    source, modes = kernel_call(
        own_modes(tables, sides),
        [places, own, x_low, x_high, smoother],
        [block(17, 16), block(400)],
        [scratch(17, 16)],
        scalars,
        flops=500_000_000,
        moved=2_000_000,
        room=8,
    )
    direction, edge, to_low, to_high = kernel_call(
        first_sweep(tables, sides),
        [places, modes, y_low, y_high, smoother],
        [block(14, 14), block(17, 8), block(4, 14), block(3, 14)],
        (),
        scalars,
        flops=2_000_000_000,
        moved=4_000_000,
        room=8,
    )
    x_low, x_high = (shift(to_high, "gx", 1), shift(to_low, "gx", -1))
    second, place_y, place_x = kernel_call(
        load_second(tables),
        [early, places, to_low],
        [
            HalfShape((tables.second_rows, 512)),
            HalfShape((tables.height + 48, 512)),
            HalfShape((16, 512)),
        ],
        [pltpu.SemaphoreType.DMA((3,))],
        {0: pl.ANY, 1: pltpu.SMEM},
        moved=6_000_000,
        room=LOADER_ROOM,
    )
    lines = [direction, x_low, x_high, second]
    to_low, to_high = kernel_call(
        edge_rows(tables),
        lines,
        [block(17, 3), block(17, 2)],
        [scratch(21, 16), scratch(21, 8), scratch(17, 8)],
        flops=500_000_000,
        moved=2_000_000,
        room=8,
    )
    y_low, y_high = (shift(to_high, "gy", 1), shift(to_low, "gy", -1))
    modes, from_b = kernel_call(
        own_rows(tables, sides),
        lines + [places, source, smoother],
        [block(400), block(16)],
        [scratch(21, 16), scratch(17, 16)],
        {4: pltpu.SMEM},
        flops=1_500_000_000,
        moved=3_000_000,
        room=8,
    )
    approx, outgoing = kernel_call(
        second_sweep(tables, sides, rho_next * rho_now, 2.0 * rho_next / delta_cheb),
        [places, direction, modes, to_low, to_high, y_low, y_high, edge, from_b]
        + [smoother, second, place_y],
        [block(14, 14), Shape((sides[1], 4, 128))],
        [scratch(17, 8), scratch(14, 16)],
        scalars,
        flops=3_000_000_000,
        moved=6_000_000,
        room=8,
    )
    arrived = lax.all_to_all(outgoing, "gy", 0, 0, tiled=True)
    (outgoing,) = kernel_call(sum_modes_y, [arrived], [Shape((sides[0], 4, 128))])
    arrived = lax.all_to_all(outgoing, "gx", 0, 0, tiled=True)
    (outgoing,) = kernel_call(
        solve_modes(tables), [arrived, late, place_x, place_y], [Shape((sides[1], 4, 128))]
    )
    arrived = lax.all_to_all(outgoing, "gy", 0, 0, tiled=True)
    correction, coarse = kernel_call(
        finish(tables, sides),
        [places, arrived, approx, late, place_y],
        [block(14, 14), Shape((2, 2, elements_z))],
        (),
        scalars,
    )
    return (correction, coarse)


def solution(mesh):
    return jax.shard_map(
        per_device,
        mesh=mesh,
        in_specs=(P("gx", "gy", None),),
        out_specs=(P("gx", "gy", None), P("gx", "gy", None)),
        check_vma=False,
    )
```

```python
import math

import jax
import jax.numpy as jnp
import ml_dtypes
import numpy as np
from jax import lax
from jax.experimental import pallas as pl
from jax.experimental.pallas import tpu as pltpu
from jax.sharding import PartitionSpec as P

theta_cheb = 1.125
delta_cheb = 0.875
start_points = [
    -0.8717401485096066,
    -0.5917001814331423,
    -0.2092992179024789,
    0.2092992179024789,
    0.5917001814331423,
    0.8717401485096066,
]


def legendre_pair(value):
    before, now = (1.0, value)
    for order in range(1, 7):
        before, now = (now, ((2 * order + 1) * value * now - order * before) / (order + 1))
    return (now, before)


def lobatto_tables():
    point_list = [-1.0]
    for guess in start_points:
        place = guess
        for newton in range(4):
            seventh, sixth = legendre_pair(place)
            slope = 7.0 * (place * seventh - sixth) / (place * place - 1.0)
            curve = (2.0 * place * slope - 56.0 * seventh) / (1.0 - place * place)
            place = place - slope / curve
        point_list.append(place)
    point_list.append(1.0)
    sample_nodes_list = np.array(point_list)
    values = np.array([legendre_pair(place)[0] for place in point_list])
    weights = 2.0 / (56.0 * values * values)
    derivative = np.zeros((8, 8))
    for i in range(8):
        for j in range(8):
            if i != j:
                derivative[i, j] = values[i] / (
                    values[j] * (sample_nodes_list[i] - sample_nodes_list[j])
                )
    derivative[0, 0] = -14.0
    derivative[7, 7] = 14.0
    stiffness = derivative.T @ (weights[:, None] * derivative)
    return (sample_nodes_list, weights, stiffness)


def assemble(elements, stiffness, weights):
    width = 7 * elements + 1
    assembled = np.zeros((width, width))
    masses = np.zeros(width)
    for e in range(elements):
        assembled[7 * e : 7 * e + 8, 7 * e : 7 * e + 8] += stiffness
        masses[7 * e : 7 * e + 8] += weights
    return (assembled, masses)


def jacobi_eigen(matrix):
    order = matrix.shape[0]
    work = [[float(matrix[i, j]) for j in range(order)] for i in range(order)]
    vectors = [[1.0 if i == j else 0.0 for j in range(order)] for i in range(order)]
    for sweep in range(12):
        for p in range(order):
            for q in range(p + 1, order):
                angle = 0.5 * math.atan2(2.0 * work[p][q], work[q][q] - work[p][p])
                cosine = math.cos(angle)
                sine = math.sin(angle)
                for k in range(order):
                    left, right = (work[k][p], work[k][q])
                    work[k][p] = cosine * left - sine * right
                    work[k][q] = sine * left + cosine * right
                for k in range(order):
                    left, right = (work[p][k], work[q][k])
                    work[p][k] = cosine * left - sine * right
                    work[q][k] = sine * left + cosine * right
                for k in range(order):
                    left, right = (vectors[k][p], vectors[k][q])
                    vectors[k][p] = cosine * left - sine * right
                    vectors[k][q] = sine * left + cosine * right
    return (np.array([work[i][i] for i in range(order)]), np.array(vectors))


def schwarz_basis():
    sample_nodes_list, weights, stiffness = lobatto_tables()
    assembled, masses = assemble(3, stiffness, weights)
    block_stiff = assembled[6:16, 6:16]
    inv_root = 1.0 / np.sqrt(masses[6:16])
    eigen_vals, eigen_vecs = jacobi_eigen(inv_root[:, None] * block_stiff * inv_root[None, :])
    return (inv_root[:, None] * eigen_vecs, eigen_vals)


def forward_table(elements, eigen_basis):
    matrix = np.zeros((10 * elements, 7 * elements + 4))
    for j in range(elements):
        matrix[10 * j : 10 * j + 10, 7 * j + 1 : 7 * j + 11] = eigen_basis.T
    return matrix


def backward_table(elements, eigen_basis):
    matrix = np.zeros((7 * elements, 10 * elements))
    for j in range(elements):
        matrix[7 * j : 7 * j + 7, 10 * j : 10 * j + 10] = eigen_basis[1:8]
    return matrix


def injection_coefficients(elements, sample_nodes_list):
    matrix = np.zeros((elements + 1, 7 * elements))
    for e in range(elements):
        for m in range(7):
            matrix[e, 7 * e + m] += (1.0 - sample_nodes_list[m]) / 2.0
            matrix[e + 1, 7 * e + m] += (1.0 + sample_nodes_list[m]) / 2.0
    return matrix


def sine_modes(vertex, elements):
    modes = np.arange(elements)
    angles = np.pi * modes / elements
    entries = np.sqrt(2.0 / elements) * np.sin(
        np.pi * (np.asarray(vertex)[:, None] * modes[None, :] % (2 * elements)) / elements
    )
    entries = entries / np.sqrt((4.0 + 2.0 * np.cos(angles)) / 3.0)[None, :]
    return np.where(modes[None, :] > 0, entries, 0.0)


def coarse_eigen(elements):
    angles = np.pi * np.arange(elements) / elements
    return np.where(
        np.arange(elements) > 0, 3.0 * (1.0 - np.cos(angles)) / (4.0 + 2.0 * np.cos(angles)), 1.0
    )


class Pack:
    def __init__(self, width):
        self.width, self.rows, self.blocks = (width, 0, [])

    def put(self, row, lane, matrix):
        self.blocks.append((row, lane, np.asarray(matrix)))
        self.rows = max(self.rows, row + -(-matrix.shape[0] // 16) * 16)
        return (slice(row, row + matrix.shape[0]), slice(lane, lane + matrix.shape[1]))

    def add(self, matrix, count=2):
        parts = []
        for _ in range(count):
            parts.append(np.asarray(matrix).astype(ml_dtypes.bfloat16))
            matrix = matrix - parts[-1].astype(np.float64)
        row, step = (self.rows, max(128, -(-matrix.shape[1] // 128) * 128))
        places = []
        for number, part in enumerate(parts):
            if step * count <= self.width:
                places.append(self.put(row, step * number, part))
            else:
                places.append(self.put(self.rows, 0, part))
        return tuple(places)

    def add_stacked(self, matrix):
        high = np.asarray(matrix).astype(ml_dtypes.bfloat16)
        low = (matrix - high.astype(np.float64)).astype(ml_dtypes.bfloat16)
        stacked = np.concatenate([high, high, low], axis=1)
        return tuple(
            self.put(self.rows, 0, stacked[:, start : start + self.width])
            for start in range(0, stacked.shape[1], self.width)
        )

    def array(self, dtype, rows=0):
        whole = np.zeros((max(self.rows, rows), self.width), dtype)
        for row, lane, matrix in self.blocks:
            whole[row : row + matrix.shape[0], lane : lane + matrix.shape[1]] = matrix
        return whole


def parts(ref, places):
    return tuple(ref[place] for place in places)


def whole(ref, places, rows=None):
    if rows is not None:
        places = [(rows, lanes) for _, lanes in places]
    high, middle, low = (ref[place].astype(jnp.float32) for place in places)
    return high + (middle + low)


def split(value):
    high = value.astype(jnp.bfloat16)
    return (high, (value - high.astype(jnp.float32)).astype(jnp.bfloat16))


def dot3(left, right):
    def mul(a, b):
        return jnp.dot(a, b, preferred_element_type=jnp.float32)

    if left[0].shape[1] % 128 == 0:
        return mul(
            jnp.concatenate([left[0], left[0], left[1]], axis=1),
            jnp.concatenate([right[0], right[1], right[0]], axis=0),
        )
    return mul(left[0], right[0]) + (mul(left[0], right[1]) + mul(left[1], right[0]))


def dot_stacked(tables, right):
    stacked = jnp.concatenate([right[0], right[1], right[0]], axis=0)
    total, start = (None, 0)
    for table in tables:
        stop = start + table.shape[1]
        part = jnp.dot(table, stacked[start:stop], preferred_element_type=jnp.float32)
        total, start = (part if total is None else total + part, stop)
    return total


def dot32(left, right):
    return jnp.dot(
        left, right, precision=lax.Precision.HIGHEST, preferred_element_type=jnp.float32
    )


NONE = None
OWN = list(range(14)) + [NONE, NONE]
X_RING = OWN[:14] + [14, 15, -1]
Y_RING = OWN + [14, 15, -1] + [NONE] * 5
EDGE = [0, 1, NONE, 13] + [NONE] * 4
VERTICES = [(0, 0), (0, 1), (1, 0), (1, 1), (0, 2), (1, 2), (2, 0), (2, 1), (2, 2)]
LOADER_ROOM = 48
EARLY_ROWS = 20 * 1024


def pick(matrix, rows, columns, row_zero, column_zero):
    result = np.zeros((len(rows), len(columns)))
    for i, row in enumerate(rows):
        for j, column in enumerate(columns):
            if row is not None and column is not None:
                result[i, j] = matrix[row + row_zero, column + column_zero]
    return result


def pick_vector(vector, slots, zero):
    return np.array([0.0 if slot is None else vector[slot + zero] for slot in slots])


class Tables:
    def __init__(self, elements_z, count_x, count_y):
        points, weights, stiffness = lobatto_tables()
        basis, values = schwarz_basis()
        nodes_z = 7 * elements_z
        half = elements_z // 2
        self.cut = cut = (7 * half) // 128 * 128
        self.first = first = min(256, nodes_z)
        self.stiffness = stiffness
        smoother, second = (Pack(512), Pack(512))
        mask_z = np.arange(nodes_z) > 0

        ahead = forward_table(2, basis)
        back = backward_table(2, basis)
        back_y = np.zeros((16, 20))
        back_y[:14] = back
        ahead_x = pick(ahead, range(20), X_RING, 0, 2)
        self.ahead_own = smoother.add_stacked(np.kron(ahead_x, pick(ahead, range(20), OWN, 0, 2)))
        ahead_edge = pick(ahead, range(20), Y_RING[16:], 0, 2)
        ahead_edge[:, 3] = -ahead[:, 2]
        ahead_edge[:, 4] = -(ahead[:, 9:16] @ stiffness[:7, 7])
        edge_table = np.zeros((400, 144))
        edge_table[:, :136] = np.kron(ahead_x, ahead_edge)
        self.ahead_edge = smoother.add_stacked(edge_table)
        self.back_xy = smoother.add_stacked(np.kron(back, back_y))
        all_ahead = forward_table(elements_z, basis)[:, 2 : 2 + nodes_z].T * mask_z[:, None]
        all_back = backward_table(elements_z, basis).T * mask_z[None, :]
        self.ahead_z, self.back_z, self.value_columns = ([], [], [])
        for low, high, base, stop in ((0, half, 0, first), (half, elements_z, cut, nodes_z)):
            modes, width = (slice(10 * low, 10 * high), 10 * (high - low))
            assert not all_ahead[:base, modes].any() and not all_ahead[stop:, modes].any()
            assert not all_back[modes, :base].any() and not all_back[modes, stop:].any()
            ahead_z, back_z = (np.zeros((stop - base, 256)), np.zeros((256, stop - base)))
            ahead_z[:, :width] = all_ahead[base:stop, modes]
            back_z[:width] = all_back[modes, base:stop]
            columns = np.ones((1, 256))
            columns[0, :width] = np.tile(values, high - low)
            self.ahead_z.append(smoother.add(ahead_z))
            self.back_z.append(smoother.add(back_z))
            self.value_columns.append(smoother.add(columns, 3))
        rows = np.add.outer(np.tile(values, 2), np.tile(values, 2)).reshape(400, 1)
        self.value_rows = smoother.add(rows, 3)

        pair, _ = assemble(2, stiffness, weights)
        _, mass = assemble(4, stiffness, weights)
        stiff_x = np.zeros((17, 21))
        stiff_x[:15, :15] = pair
        stiff_x[0, 0] += stiffness[7, 7]
        stiff_x[16, 0] = stiffness[6, 7]
        for row, column in ((0, 17), (16, 18), (14, 19), (15, 20)):
            stiff_x[row, column] = 1.0
        stiff_y = np.zeros((16, 16))
        stiff_y[:14, :14] = pair[:14, :14]
        stiff_y[0, 0] += stiffness[7, 7]
        edge_y = np.zeros((8, 16))
        edge_y[0, 0:8], edge_y[1, 0:8], edge_y[2, 0] = (stiffness[0], stiffness[1], 1.0)
        edge_y[3, 7:14], edge_y[4, 7:14] = (stiffness[6, :7], stiffness[7, :7])
        mass_x, mass_y = (pick_vector(mass, X_RING, 7), pick_vector(mass, OWN, 7))
        mass_edge = pick_vector(mass, EDGE, 7)
        batches = ((0, 8), (8, 16), (16, 17))
        self.batches = batches
        self.edge_x = second.add(np.kron(stiff_x, np.diag(mass_edge)))
        self.edge_y = [
            second.add(np.kron(np.diag(mass_x[low:high]), edge_y)) for low, high in batches
        ]
        self.own_x = [
            second.add(np.kron(stiff_x, np.diag(mass_y[low : low + 8]))) for low in (0, 8)
        ]
        self.own_y = [
            second.add(np.kron(np.diag(mass_x[low:high]), stiff_y)) for low, high in batches
        ]
        self.mass_edge = second.add(np.outer(mass_x, mass_edge).reshape(-1, 1), 3)
        self.mass_own = second.add(np.outer(mass_x, mass_y).reshape(-1, 1), 3)
        stiff_z, line_z = assemble(elements_z, stiffness, weights)
        stiff_z, line_z = (stiff_z[:nodes_z, :nodes_z], line_z[:nodes_z])
        self.mass_z = second.add(line_z[None, :], 3)
        low_z, high_z = (stiff_z[:first, :first].copy(), stiff_z[cut:, cut:].copy())
        low_z[:, 7 * half :] = 0.0
        high_z[:, : 7 * half - cut] = 0.0
        self.stiff_z = [second.add(low_z), second.add(high_z)]

        stiff3, mass3 = assemble(3, stiffness, weights)
        inject = np.zeros((4, 22))
        inject[:, :21] = injection_coefficients(3, points)
        inject[3, 21] = 1.0

        def padded(matrix):
            wide = np.zeros((matrix.shape[0], 16))
            wide[:, :14] = matrix
            return wide

        drop = inject[:, 7:21]
        drop_mass = (inject * mass3[None, :])[:, 7:21]
        drop_stiff = (inject @ stiff3)[:, 7:21]
        self.drop_b = second.add(np.kron(drop, padded(drop)))
        across = np.kron(drop_stiff, padded(drop_mass)) + np.kron(drop_mass, padded(drop_stiff))
        drop_x = -np.concatenate([across, np.kron(drop_mass, padded(drop_mass))])
        self.drop_x = second.add(drop_x)
        whole_back = np.kron(back, back_y)
        self.drop_modes = []
        for below_x in (0.0, 1.0):
            for below_y in (0.0, 1.0):
                mask = np.ones((14, 16))
                mask[0] *= below_x
                mask[:, 0] *= below_y
                self.drop_modes.append(second.add((drop_x * mask.reshape(1, 224)) @ whole_back))
        drop_z = injection_coefficients(elements_z, points)[:elements_z]
        phi_z = sine_modes(np.arange(elements_z), elements_z)
        masked_z = (drop_z * mask_z[None, :]).T
        modes_z = np.zeros((nodes_z, 384))
        for part, matrix in enumerate((masked_z, line_z[:, None] * masked_z, stiff_z @ masked_z)):
            for base in (128 * part, 128 * part + 64):
                modes_z[:, base : base + elements_z] = matrix @ phi_z
        self.modes_z = second.add(modes_z)

        sides_x, sides_y = (count_x // 2, count_y // 2)
        phi_x = sine_modes(np.arange(count_x + 1), count_x)
        phi_y = sine_modes(np.arange(count_y + 1), count_y)
        lam_x, lam_y = (coarse_eigen(count_x), coarse_eigen(count_y))
        assert elements_z <= 64 and sides_y <= 16
        eigen_z = coarse_eigen(elements_z)
        eye_x = np.eye(4)
        to_y = np.zeros((sides_y, sides_y, 4, 2, 4, 4))
        from_y = np.zeros((sides_y, 2, 16, sides_y, 4))
        eigen_yz = np.ones((sides_y, 2, 64))
        for place in range(sides_y):
            eigen_yz[place, :, :elements_z] = (
                lam_y[2 * place : 2 * place + 2, None] + eigen_z[None, :]
            )
            for j in range(4):
                if 2 * place + j - 1 >= 0:
                    row = phi_y[2 * place + j - 1].reshape(sides_y, 2)
                    to_y[place, :, :, :, :, j] = (
                        eye_x[None, :, None, :] * row[:, None, :, None]
                    )
            for number, (i, j) in enumerate(VERTICES):
                row = phi_y[2 * place + j].reshape(sides_y, 2)
                from_y[place, :, number, :, i] = row.T
        to_x = np.zeros((count_x, sides_x, 4))
        from_x = np.zeros((sides_x, 16, count_x))
        for place in range(sides_x):
            for i in range(4):
                if 2 * place + i - 1 >= 0:
                    to_x[:, place, i] = phi_x[2 * place + i - 1]
            from_x[place, :3] = phi_x[2 * place : 2 * place + 3]
        lift = injection_coefficients(2, points)
        lift_xy = np.zeros((14, 16, 16))
        for number, (i, j) in enumerate(VERTICES):
            lift_xy[:, :14, number] = np.outer(lift[i], lift[j])
        lift_xy = lift_xy.reshape(224, 16)
        self.sent = sent = 4 * sides_y
        self.count_x = count_x
        height = -(-sent // 16) * 16
        places = Pack(512)
        for place in range(sides_y):
            rows = np.zeros((height + 272, 128))
            rows[:sent, :32] = to_y[place].reshape(sent, 32)
            rows[height : height + 32, :sent] = from_y[place].reshape(32, sent)
            rows[height + 32] = eigen_yz[place].ravel()
            for half_mode in range(2):
                lanes = slice(64 * half_mode, 64 * half_mode + sent)
                rows[height + 48 :, lanes] = lift_xy @ from_y[place, half_mode].reshape(16, sent)
            places.add(rows, 3)
        self.height = height
        self.place_x_base = places.rows
        for place in range(sides_x):
            rows = np.zeros((16, 128))
            rows[:, :count_x] = from_x[place]
            places.add(rows, 3)
        lift_z, back_phi = (np.zeros((128, nodes_z)), np.zeros((128, elements_z)))
        for base in (0, 64):
            lift_z[base : base + elements_z] = phi_z.T @ drop_z * mask_z[None, :]
            back_phi[base : base + elements_z] = phi_z.T
        self.lift_z = second.add(lift_z)
        self.phi_z = second.add(back_phi)
        late = Pack(256)
        self.to_modes_x = late.put(0, 0, to_x.reshape(count_x, 4 * sides_x))
        self.eigen_x = late.put(0, 128, lam_x[:, None])
        self.late = late.array(np.float32)
        self.smoother_rows, self.second_rows = (smoother.rows, second.rows)
        self.places_base = smoother.rows + second.rows
        self.early = np.zeros((EARLY_ROWS, 512), ml_dtypes.bfloat16)
        stacked = [pack.array(ml_dtypes.bfloat16) for pack in (smoother, second, places)]
        used = np.concatenate(stacked)
        self.early[: used.shape[0]] = used
        self.place_parts = tuple(
            (slice(None), slice(128 * part, 128 * part + 128)) for part in range(3)
        )


def here():
    return (lax.axis_index("gx"), lax.axis_index("gy"))


def sides_of(places, sides):
    flags = []
    for axis in range(2):
        flags.append(jnp.where(places[axis] > 0, 1.0, 0.0))
        flags.append(jnp.where(places[axis] < sides[axis] - 1, 1.0, 0.0))
    return flags


def line_mask(flags):
    x = lax.broadcasted_iota(jnp.int32, (17, 16, 1), 0)
    y = lax.broadcasted_iota(jnp.int32, (17, 16, 1), 1)
    keep_x = jnp.where((x == 0) | (x == 16), flags[0], jnp.where(x >= 14, flags[1], 1.0))
    return keep_x * jnp.where(y == 0, flags[2], 1.0)


def edge_mask(flags):
    x = lax.broadcasted_iota(jnp.int32, (17, 8, 1), 0)
    slot = lax.broadcasted_iota(jnp.int32, (17, 8, 1), 1)
    keep_x = jnp.where((x == 0) | (x == 16), flags[0], jnp.where(x >= 14, flags[1], 1.0))
    return keep_x * jnp.where((slot == 2) | (slot == 3), flags[2], flags[3])


def own_mask(flags):
    x = lax.broadcasted_iota(jnp.int32, (14, 16, 1), 0)
    y = lax.broadcasted_iota(jnp.int32, (14, 16, 1), 1)
    return jnp.where(x == 0, flags[0], 1.0) * jnp.where(y == 0, flags[2], 1.0)


def join_z(low, high, cut):
    middle = low.shape[1]
    return jnp.concatenate(
        [low[:, :cut], low[:, cut:] + high[:, : middle - cut], high[:, middle - cut :]], axis=1
    )


def schwarz(modes, edge, inverse, tables, smoother):
    cut = tables.cut
    nodes_z = edge.shape[2]
    edge = jnp.concatenate(
        [edge.reshape(136, nodes_z), jnp.zeros((8, nodes_z), jnp.float32)], axis=0
    )
    modes = modes + dot_stacked(parts(smoother, tables.ahead_edge), split(edge))
    halves = []
    for number, block in enumerate((modes[:, : tables.first], modes[:, cut:])):
        block = dot3(split(block), parts(smoother, tables.ahead_z[number]))
        block = block * inverse[:, 256 * number : 256 * number + 256]
        halves.append(dot3(split(block), parts(smoother, tables.back_z[number])))
    lines = split(join_z(*halves, cut))
    return (lines, dot_stacked(parts(smoother, tables.back_xy), lines))


class Shape(tuple):
    dtype = jnp.float32


class HalfShape(Shape):
    dtype = jnp.bfloat16


def kernel_call(
    body, inputs, outputs, scratch=(), spaces={}, to=pltpu.VMEM, flops=0, moved=0, room=4
):
    def kernel(*refs):
        last = len(inputs) + len(outputs)
        body(refs[: len(inputs)], refs[len(inputs) : last], refs[last:])

    return pl.pallas_call(
        kernel,
        out_shape=[jax.ShapeDtypeStruct(shape, shape.dtype) for shape in outputs],
        in_specs=[
            pl.BlockSpec(memory_space=spaces.get(number, pltpu.VMEM))
            for number in range(len(inputs))
        ],
        out_specs=[pl.BlockSpec(memory_space=to) for _ in outputs],
        scratch_shapes=list(scratch),
        compiler_params=pltpu.CompilerParams(vmem_limit_bytes=room * 1024 * 1024),
        cost_estimate=pl.CostEstimate(flops=flops, bytes_accessed=moved, transcendentals=0),
    )(*inputs)


def run_copies(pairs, semaphores):
    copies = [
        pltpu.make_async_copy(source, target, semaphores.at[number])
        for number, (source, target) in enumerate(pairs)
    ]
    for copy in copies:
        copy.start()
    for copy in copies:
        copy.wait()


def load_smoother(tables):
    def body(ins, outs, scratch):
        run_copies([(ins[0].at[0 : tables.smoother_rows], outs[0])], scratch[0])

    return body


def load_second(tables):
    def body(ins, outs, scratch):
        early, _ = ins
        places = here()
        base = tables.smoother_rows
        size = tables.height + 272
        row_y = pl.multiple_of(tables.places_base + size * places[1], 16)
        row_x = pl.multiple_of(tables.places_base + tables.place_x_base + 16 * places[0], 16)
        run_copies(
            [
                (early.at[base : base + tables.second_rows], outs[0]),
                (early.at[pl.ds(row_y, size)], outs[1]),
                (early.at[pl.ds(row_x, 16)], outs[2]),
            ],
            scratch[0],
        )

    return body


def by_partner(first, second, act):
    even = lax.rem(here()[0], 2) == 0
    pl.when(even)(lambda: act(first, second))
    pl.when(jnp.logical_not(even))(lambda: act(second, first))


def first_x_rows(ins, outs, scratch):
    (own,) = ins
    outs[0][...] = own[...]

    def write(low, high):
        low[...] = own[0:2]
        high[...] = own[12:14]

    by_partner(outs[1], outs[2], write)


def first_y_rows(ins, outs, scratch):
    own, first, second, _ = ins
    blocks = tuple(zip(outs, (slice(0, 2), slice(13, 14))))
    for out, rows in blocks:
        out[0:14] = own[:, rows]

    def write(low, high):
        for out, rows in blocks:
            out[14:16] = high[:, rows]
            out[16:17] = low[1:2, rows]

    by_partner(first, second, write)


def own_modes(tables, sides):
    def body(ins, outs, scratch):
        own, first, second, smoother = ins
        (line,) = scratch
        nodes_z = own.shape[2]
        line[:, 14:16] = jnp.zeros((17, 2, nodes_z), jnp.float32)
        line[0:14, 0:14] = own[...]

        def write(low, high):
            line[14:16, 0:14] = high[...]
            line[16:17, 0:14] = low[1:2]

        by_partner(first, second, write)
        masked = line[...] * line_mask(sides_of(here(), sides))
        outs[0][...] = masked
        rows = split(masked.reshape(272, nodes_z))
        outs[1][...] = dot_stacked(parts(smoother, tables.ahead_own), rows)
        rows = whole(smoother, tables.value_rows)
        for number, columns in enumerate(tables.value_columns):
            outs[2][:, 256 * number : 256 * number + 256] = 1.0 / (rows + whole(smoother, columns))

    return body


def first_sweep(tables, sides):
    def body(ins, outs, scratch):
        modes, y_low, y_high, inverse, smoother = ins
        flags = sides_of(here(), sides)
        nodes_z = modes.shape[1]
        edge = outs[1]
        edge[:, 0:2] = y_high[...]
        edge[:, 2:3] = y_low[...]
        edge[:, 3:8] = jnp.zeros((17, 5, nodes_z), jnp.float32)
        edge[...] = edge[...] * edge_mask(flags)
        _, result = schwarz(modes[...], edge[...], inverse, tables, smoother)
        result = result.reshape(14, 16, nodes_z) * (own_mask(flags) * (1.0 / theta_cheb))
        result = result[:, :14]
        outs[0][...] = result
        stiffness = tables.stiffness
        sums = []
        for row in range(2):
            sums.append(sum(float(stiffness[row, j]) * result[j] for j in range(8)))
            sums.append(sum(float(stiffness[7 - row, j]) * result[7 + j] for j in range(7)))

        def write(low, high):
            low[0:2] = result[0:2]
            low[2], low[3] = (sums[0], sums[2])
            high[0], high[1], high[2] = (result[13], sums[1], sums[3])
            high[3] = jnp.zeros_like(result[0])

        by_partner(outs[2], outs[3], write)

    return body


def fill_lines(line, own, first, second, sides):
    flags = sides_of(here(), sides)
    line[:, 14:16] = jnp.zeros((21, 2, own.shape[2]), jnp.float32)
    line[0:14, 0:14] = own[...]

    def write(low, high):
        line[14:16, 0:14] = high[0:2] * flags[1]
        line[16:19, 0:14] = low[0:3] * flags[0]
        line[19:21, 0:14] = high[2:4] * flags[1]

    by_partner(first, second, write)


def apply_z(rows, tables, second):
    return join_z(
        dot3(split(rows[:, : tables.first]), parts(second, tables.stiff_z[0])),
        dot3(split(rows[:, tables.cut :]), parts(second, tables.stiff_z[1])),
        tables.cut,
    )


def edge_rows(tables, sides):
    def body(ins, outs, scratch):
        own, x_first, x_second, second = ins
        line, edge, total = scratch
        nodes_z = own.shape[2]
        fill_lines(line, own, x_first, x_second, sides)
        edge[...] = jnp.zeros((21, 8, nodes_z), jnp.float32)
        edge[:, 0:2] = line[:, 0:2]
        edge[:, 3:4] = line[:, 13:14]
        part = dot3(parts(second, tables.edge_x), split(edge[...].reshape(168, nodes_z)))
        total[...] = part.reshape(17, 8, nodes_z)
        for places, (low, high) in zip(tables.edge_y, tables.batches):
            rows = line[low:high].reshape(16 * (high - low), nodes_z)
            part = dot3(parts(second, places), split(rows))
            total[low:high] += part.reshape(high - low, 8, nodes_z)
        along = apply_z(edge[0:17].reshape(136, nodes_z), tables, second)
        result = total[...].reshape(136, nodes_z) * whole(second, tables.mass_z)
        result = result + whole(second, tables.mass_edge) * along
        total[...] = result.reshape(17, 8, nodes_z)
        outs[0][...] = total[:, 0:3]
        outs[1][...] = total[:, 3:5]

    return body


def own_rows(tables, sides, scale_old):
    def body(ins, outs, scratch):
        own, x_first, x_second, second, source, smoother = ins
        line, total = scratch
        modes, from_b = outs
        nodes_z = own.shape[2]
        fill_lines(line, own, x_first, x_second, sides)
        for number, place in enumerate(tables.own_x):
            rows = line[:, 8 * number : 8 * number + 8].reshape(168, nodes_z)
            part = dot3(parts(second, place), split(rows))
            total[:, 8 * number : 8 * number + 8] = part.reshape(17, 8, nodes_z)
        for place, (low, high) in zip(tables.own_y, tables.batches):
            rows = line[low:high].reshape(16 * (high - low), nodes_z)
            part = dot3(parts(second, place), split(rows))
            total[low:high] += part.reshape(high - low, 16, nodes_z)
        along = apply_z(line[0:17].reshape(272, nodes_z), tables, second)
        applied = total[...].reshape(272, nodes_z) * whole(second, tables.mass_z)
        applied = applied + whole(second, tables.mass_own) * along
        remain = (source[...] - applied.reshape(17, 16, nodes_z)) * line_mask(sides_of(here(), sides))
        remain = split(remain.reshape(272, nodes_z))
        modes[...] = dot_stacked(parts(smoother, tables.ahead_own), remain)
        rows = source[0:14].reshape(224, nodes_z)
        from_b[0:16] = dot3(parts(second, tables.drop_b), split(rows))
        rows = (1.0 + scale_old) * line[0:14].reshape(224, nodes_z)
        from_b[16:48] = dot3(parts(second, tables.drop_x), split(rows))

    return body


def second_sweep(tables, sides, scale_old, scale_new):
    def body(ins, outs, scratch):
        own, modes, to_low, to_high, y_low, y_high, source, from_b = ins[:8]
        inverse, smoother, second, place_y = ins[8:]
        (edge,) = scratch
        flags = sides_of(here(), sides)
        nodes_z = own.shape[2]
        stiffness = tables.stiffness
        above = y_high[:, 2:3]
        edge[:, 0:1] = source[:, 0:1] - (
            y_high[:, 0:1] + to_high[:, 1:2] + float(stiffness[7, 7]) * above
        )
        edge[:, 1:2] = source[:, 1:2] - y_high[:, 1:2]
        edge[:, 2:3] = source[:, 2:3] - (y_low[:, 0:1] + float(stiffness[6, 7]) * to_low[:, 2:3])
        edge[:, 3:4] = y_low[:, 1:2]
        edge[:, 4:5] = above
        edge[:, 5:8] = jnp.zeros((17, 3, nodes_z), jnp.float32)
        lines, result = schwarz(modes[...], edge[...] * edge_mask(flags), inverse, tables, smoother)
        below_x, _, below_y, _ = flags
        number = jnp.where(below_x > 0.0, 2, 0) + jnp.where(below_y > 0.0, 1, 0)
        (rows, lanes), (more, _) = tables.drop_modes[0]
        step = tables.drop_modes[1][0][0].start - rows.start
        drop = tuple(
            second[pl.ds(pl.multiple_of(part.start + step * number, 16), 32), lanes]
            for part in (rows, more)
        )
        from_x = scale_new * dot3(drop, lines)
        both = jnp.concatenate([from_b[0:16], from_b[16:48] + from_x], axis=0)
        result = result.reshape(14, 16, nodes_z) * (own_mask(flags) * scale_new)
        outs[0][...] = (1.0 + scale_old) * own[...] + result[:, 0:14]
        modes = dot3(split(both), parts(second, tables.modes_z))
        modes = modes[0:16, 0:128] + modes[16:32, 128:256] + modes[32:48, 256:384]
        left = lax.broadcasted_iota(jnp.int32, (16, 128), 1) < 64
        modes = jnp.concatenate([jnp.where(left, modes, 0.0), jnp.where(left, 0.0, modes)], axis=0)
        to_modes_y = [part[0 : tables.sent, 0:32] for part in parts(place_y, tables.place_parts[:2])]
        outs[1][...] = dot3(to_modes_y, split(modes)).reshape(outs[1].shape)

    return body


def sum_modes_y(ins, outs, scratch):
    outs[0][...] = jnp.broadcast_to(jnp.sum(ins[0][...], axis=0, keepdims=True), outs[0].shape)


def solve_modes(tables):
    def body(ins, outs, scratch):
        arrived, late, place_x, place_y = ins
        modes = dot32(late[tables.to_modes_x], arrived[...].reshape(-1, 128))
        row = tables.height + 32
        eigen_yz = whole(place_y, tables.place_parts, slice(row, row + 16))[0:1]
        modes = modes / (late[tables.eigen_x] + eigen_yz)
        back = dot32(whole(place_x, tables.place_parts)[0:8, 0 : tables.count_x], modes)
        outs[0][...] = jnp.broadcast_to(back[None, 0:4], outs[0].shape)

    return body


def finish(tables, sides):
    def body(ins, outs, scratch):
        arrived, approx, second, place_y = ins
        sums, vertices_out, semaphores = scratch
        nodes_z = approx.shape[2]
        rows = arrived[...].reshape(-1, 128)
        left = lax.broadcasted_iota(jnp.int32, rows.shape, 1) < 64
        lines = jnp.concatenate([jnp.where(left, rows, 0.0), jnp.where(left, 0.0, rows)], axis=0)
        if tables.sent < 64:
            empty = jnp.zeros((64 - tables.sent, 128), jnp.float32)
            lines = jnp.concatenate(
                [lines[: tables.sent], empty, lines[tables.sent :], empty], axis=0
            )
        lines = dot3(split(lines), parts(second, tables.lift_z))
        back = slice(tables.height, tables.height + 32)
        back = [place_y[back, lanes][:, 0 : tables.sent] for _, lanes in tables.place_parts[:2]]
        vertices = dot3(back, split(rows))
        left = lax.broadcasted_iota(jnp.int32, (16, 128), 1) < 64
        vertices = split(jnp.where(left, vertices[0:16], vertices[16:32]))
        coarse = dot3(vertices, parts(second, tables.phi_z))
        vertices_out[0] = coarse[0:2]
        vertices_out[1] = coarse[2:4]
        copies = [pltpu.make_async_copy(vertices_out, outs[1], semaphores.at[2])]
        copies[0].start()
        lines = split(lines)
        mask = own_mask(sides_of(here(), sides))
        base = tables.height + 48
        for number, (low, high) in enumerate(((0, 7), (7, 14))):
            lift = slice(base + 16 * low, base + 16 * high)
            lift = tuple(place_y[lift, lanes] for _, lanes in tables.place_parts[:2])
            fine = dot3(lift, lines).reshape(high - low, 16, nodes_z) * mask[low:high]
            sums[low:high] = approx[low:high] + fine[:, :14]
            copies.append(
                pltpu.make_async_copy(
                    sums.at[low:high], outs[0].at[low:high], semaphores.at[number]
                )
            )
            copies[-1].start()
        for copy in copies:
            copy.wait()

    return body


def shift_y(block, distance):
    count = lax.axis_size("gy")
    return lax.ppermute(block, "gy", [((i - distance) % count, i) for i in range(count)])


def swap_x(first, second):
    count = lax.axis_size("gx")
    assert count % 2 == 0
    across = [(i, (i + 1 if i % 2 else i - 1) % count) for i in range(count)]
    within = [(i, i ^ 1) for i in range(count)]
    return (lax.ppermute(first, "gx", across), lax.ppermute(second, "gx", within))


def per_device(residual_in):
    nodes_x, nodes_y, nodes_z = residual_in.shape
    assert nodes_x == 14 and nodes_y == 14 and nodes_z % 14 == 0
    sides = (lax.axis_size("gx"), lax.axis_size("gy"))
    elements_z = nodes_z // 7
    tables = Tables(elements_z, 2 * sides[0], 2 * sides[1])
    early, late = (jnp.asarray(tables.early), jnp.asarray(tables.late))
    sigma_ratio = theta_cheb / delta_cheb
    rho_now = 1.0 / sigma_ratio
    rho_next = 1.0 / (2.0 * sigma_ratio - rho_now)

    def block(*shape):
        return Shape(shape + (nodes_z,))

    def scratch(*shape):
        return pltpu.VMEM(shape + (nodes_z,), jnp.float32)

    own, to_first, to_second = kernel_call(
        first_x_rows,
        [residual_in],
        [block(14, 14), block(2, 14), block(2, 14)],
    )
    x_first, x_second = swap_x(to_first, to_second)
    (smoother,) = kernel_call(
        load_smoother(tables),
        [early],
        [HalfShape((tables.smoother_rows, 512))],
        [pltpu.SemaphoreType.DMA((1,))],
        {0: pl.ANY},
        moved=6_000_000,
        room=LOADER_ROOM,
    )
    to_low, to_high = kernel_call(
        first_y_rows,
        [own, x_first, x_second, smoother],
        [block(17, 2), block(17, 1)],
    )
    y_low, y_high = (shift_y(to_high, 1), shift_y(to_low, -1))
    source, modes, inverse = kernel_call(
        own_modes(tables, sides),
        [own, x_first, x_second, smoother],
        [block(17, 16), block(400), Shape((400, 512))],
        [scratch(17, 16)],
        flops=500_000_000,
        moved=2_000_000,
        room=8,
    )
    direction, edge, to_first, to_second = kernel_call(
        first_sweep(tables, sides),
        [modes, y_low, y_high, inverse, smoother],
        [block(14, 14), block(17, 8), block(4, 14), block(4, 14)],
        flops=2_000_000_000,
        moved=4_000_000,
        room=8,
    )
    x_first, x_second = swap_x(to_first, to_second)
    second, place_y, place_x = kernel_call(
        load_second(tables),
        [early, to_first],
        [
            HalfShape((tables.second_rows, 512)),
            HalfShape((tables.height + 272, 512)),
            HalfShape((16, 512)),
        ],
        [pltpu.SemaphoreType.DMA((3,))],
        {0: pl.ANY},
        moved=6_000_000,
        room=LOADER_ROOM,
    )
    lines = [direction, x_first, x_second, second]
    to_low, to_high = kernel_call(
        edge_rows(tables, sides),
        lines,
        [block(17, 3), block(17, 2)],
        [scratch(21, 16), scratch(21, 8), scratch(17, 8)],
        flops=500_000_000,
        moved=2_000_000,
        room=8,
    )
    y_low, y_high = (shift_y(to_high, 1), shift_y(to_low, -1))
    modes, from_b = kernel_call(
        own_rows(tables, sides, rho_next * rho_now),
        lines + [source, smoother],
        [block(400), block(48)],
        [scratch(21, 16), scratch(17, 16)],
        flops=1_500_000_000,
        moved=3_000_000,
        room=8,
    )
    approx, outgoing = kernel_call(
        second_sweep(tables, sides, rho_next * rho_now, 2.0 * rho_next / delta_cheb),
        [direction, modes, to_low, to_high, y_low, y_high, edge, from_b]
        + [inverse, smoother, second, place_y],
        [block(14, 14), Shape((sides[1], 4, 128))],
        [scratch(17, 8)],
        flops=3_000_000_000,
        moved=6_000_000,
        room=8,
    )
    arrived = lax.all_to_all(outgoing, "gy", 0, 0, tiled=True)
    (outgoing,) = kernel_call(sum_modes_y, [arrived], [Shape((sides[0], 4, 128))])
    arrived = lax.all_to_all(outgoing, "gx", 0, 0, tiled=True)
    (outgoing,) = kernel_call(
        solve_modes(tables), [arrived, late, place_x, place_y], [Shape((sides[1], 4, 128))]
    )
    arrived = lax.all_to_all(outgoing, "gy", 0, 0, tiled=True)
    correction, coarse = kernel_call(
        finish(tables, sides),
        [arrived, approx, second, place_y],
        [block(14, 14), Shape((2, 2, elements_z))],
        [
            scratch(14, 14),
            pltpu.VMEM((2, 2, elements_z), jnp.float32),
            pltpu.SemaphoreType.DMA((3,)),
        ],
        to=pl.ANY,
    )
    return (correction, coarse)


def solution(mesh):
    return jax.shard_map(
        per_device,
        mesh=mesh,
        in_specs=(P("gx", "gy", None),),
        out_specs=(P("gx", "gy", None), P("gx", "gy", None)),
        check_vma=False,
    )
```
